32 devices in a mesh: tok: 4 (over y, x), chan: 8 (over z, core).
Axes of the slice: x: 2, y: 2, z: 4, core: 2. Of those that a mesh axis runs over, the one named last changes fastest.
Arguments:
- acts: bfloat16 [2048, 28672], P('tok', 'chan'), may hold values from -6 to 6
- target: bfloat16 [2048, 8192], P('tok', 'chan'), may hold values from -6 to 6
- proj_b: bfloat16 [2048, 28672], P(None, 'chan'), may hold values from -0.03125 to 0.03125
- proj_a: bfloat16 [8192, 2048], P('chan'), may hold values from -0.125 to 0.125
Outputs:
- grad_a: float32 [8192, 2048], P('chan', 'tok')
- grad_b: float32 [2048, 28672], P('tok', 'chan')
The draws below stay inside these ranges and needn't reach their ends.
All inputs are finite; a program needn't handle non-finite values.
Results may differ from the reference program's by a relative error of at most 0.004.
Values may be sent and summed in bfloat16 or wider, within the bound.
A program may use at most 192 MiB of HBM per device.

```python
import jax
import jax.numpy as jnp
from jax import lax

IN = 28672
OUT = 8192
RANK = 2048
TOKENS = 2048


def block_levels(key, shape, pieces, least, largest):
    level, own = 1.0, jax.random.fold_in(key, 6)
    for position, shards_of in pieces:
        draws = jnp.exp(jax.random.uniform(jax.random.fold_in(own, position), (shards_of,), jnp.float32, least / len(pieces), largest / len(pieces)))
        level = level * jnp.repeat(draws, shape[position] // shards_of).reshape([-1 if axis == position else 1 for axis in range(len(shape))])
    return level


def bell_draw(stream_key, extent, spread, bound, cuts=(), dtype=jnp.bfloat16):
    factor_of = block_levels(stream_key, extent, cuts, -0.22, 0.18) if cuts else 1.0
    values = jax.random.normal(stream_key, extent, jnp.float32) * spread * factor_of
    return jnp.minimum(jnp.maximum(values, -bound), bound).astype(dtype)


def setup_inputs(seed: int = 0) -> dict:
    seeds = jax.random.split(jax.random.key(seed), 5)
    acts = bell_draw(seeds[0], (TOKENS, IN), 1.0, 6.0, ((0, 4), (1, 8)))
    target = bell_draw(seeds[1], (TOKENS, OUT), 1.0, 6.0, ((0, 4), (1, 8)))
    proj_b = bell_draw(seeds[2], (RANK, IN), IN ** -0.5, 0.03125, ((1, 8),))
    proj_a = bell_draw(seeds[3], (OUT, RANK), RANK ** -0.5, 0.125, ((0, 8),))
    return {"acts": acts, "target": target, "proj_b": proj_b, "proj_a": proj_a}


def reference(acts, target, proj_b, proj_a):
    codes = lax.dot_general(acts, proj_b, (((1,), (1,)), ((), ())), preferred_element_type=jnp.float32).astype(jnp.bfloat16)
    predicted = lax.dot_general(codes, proj_a, (((1,), (1,)), ((), ())), preferred_element_type=jnp.float32)
    residual = (target.astype(jnp.float32) - predicted).astype(jnp.bfloat16)
    grad_codes = jnp.dot(residual, proj_a, preferred_element_type=jnp.float32).astype(jnp.bfloat16)
    factor_scale = -2.0 / TOKENS
    grad_a = lax.dot_general(residual, codes, (((0,), (0,)), ((), ())), preferred_element_type=jnp.float32) * factor_scale
    grad_b = lax.dot_general(grad_codes, acts, (((0,), (0,)), ((), ())), preferred_element_type=jnp.float32) * factor_scale
    return grad_a, grad_b
```

```python
import functools

import jax
import jax.numpy as jnp
from jax import lax
from jax.experimental import pallas as pl
from jax.experimental.pallas import tpu as pltpu
from jax.sharding import PartitionSpec as P

MESH = pl.DeviceIdType.MESH


def reduce_gather_kernel(
    chips, groups, x_ref, out_ref, pair, mine, slots, reduced, total,
    pair_send, pair_recv, rs_send, rs_recv, tok_send, tok_recv,
    ag_send, ag_recv, fwd_send, fwd_recv,
):
    me = lax.axis_index("chan")
    chip, core = me // 2, me % 2
    other = 1 - core
    partner = chip * 2 + other
    tok = lax.axis_index("tok")

    def peer(step):
        return lax.rem(chip + step, chips)

    def group(step):
        return lax.rem(tok + step, groups)

    barrier = pltpu.get_barrier_semaphore()
    pl.semaphore_signal(barrier, inc=1, device_id={"chan": partner}, device_id_type=MESH)
    for step in range(1, chips):
        pl.semaphore_signal(
            barrier, inc=1, device_id={"chan": peer(step) * 2 + core}, device_id_type=MESH
        )
    for step in range(1, groups):
        pl.semaphore_signal(barrier, inc=1, device_id={"tok": group(step)}, device_id_type=MESH)
    pl.semaphore_wait(barrier, chips + groups - 1)

    order = [(chips // 2 + step) % chips for step in range(chips)]
    order = [step for step in order if step] + [0]

    def pair_copy(step):
        slot = peer(step)
        return pltpu.make_async_remote_copy(
            x_ref.at[:, other, slot], pair.at[slot], pair_send.at[slot], pair_recv.at[slot],
            device_id={"chan": partner}, device_id_type=MESH,
        )

    for step in order:
        pair_copy(step).start()

    def rs_copy(step, landed):
        slot = peer(step)
        return pltpu.make_async_remote_copy(
            mine.at[slot], slots.at[landed], rs_send.at[slot], rs_recv.at[landed],
            device_id={"chan": slot * 2 + core}, device_id_type=MESH,
        )

    for step in order:
        slot = peer(step)
        pair_copy(step).wait_recv()
        value = x_ref[:, core, slot] + pair[slot]
        if step:
            mine[slot] = value.astype(jnp.bfloat16)
            rs_copy(step, chip).start()
        else:
            total[...] = value
    for step in range(1, chips):
        slot = peer(step)
        rs_copy(step, slot).wait_recv()
        total[...] += slots[slot].astype(jnp.float32)

    if groups == 1:
        out_ref[:, core, chip] = total[...].astype(jnp.bfloat16)
    else:
        reduced[...] = total[...].astype(jnp.bfloat16)

        def tok_copy(step, landed):
            target = group(step)
            return pltpu.make_async_remote_copy(
                reduced.at[target], out_ref.at[landed, core, chip],
                tok_send.at[target], tok_recv.at[landed],
                device_id={"tok": target}, device_id_type=MESH,
            )

        for step in range(1, groups):
            tok_copy(step, tok).start()
        out_ref[tok, core, chip] = reduced[tok]
        for step in range(1, groups):
            tok_copy(step, group(step)).wait_recv()

    def ag_copy(step, landed):
        block = out_ref.at[:, core, landed]
        slot = peer(step)
        return pltpu.make_async_remote_copy(
            block, block, ag_send.at[slot], ag_recv.at[landed],
            device_id={"chan": slot * 2 + core}, device_id_type=MESH,
        )

    def fwd_copy(slot, side):
        block = out_ref.at[:, side, slot]
        return pltpu.make_async_remote_copy(
            block, block, fwd_send.at[slot], fwd_recv.at[slot],
            device_id={"chan": partner}, device_id_type=MESH,
        )

    for step in order[:-1]:
        ag_copy(step, chip).start()
    fwd_copy(chip, core).start()
    for step in range(1, chips):
        slot = peer(step)
        ag_copy(step, slot).wait_recv()
        fwd_copy(slot, core).start()
    for step in range(chips):
        fwd_copy(peer(step), other).wait_recv()

    for step in range(chips):
        pair_copy(step).wait_send()
        fwd_copy(peer(step), core).wait_send()
        if step:
            rs_copy(step, chip).wait_send()
            ag_copy(step, chip).wait_send()
    if groups > 1:
        for step in range(1, groups):
            tok_copy(step, tok).wait_send()


def reduce_gather(x, devices, groups, collective_id):
    rows, tokens = x.shape
    chips = devices // 2
    part = rows // (devices * groups)
    shape = (groups, 2, chips, part, tokens)
    block = (groups, part, tokens)
    vmem = pl.BlockSpec(memory_space=pltpu.VMEM)
    dma = pltpu.SemaphoreType.DMA
    return pl.pallas_call(
        functools.partial(reduce_gather_kernel, chips, groups),
        out_shape=jax.ShapeDtypeStruct(shape, jnp.bfloat16),
        in_specs=[vmem],
        out_specs=vmem,
        scratch_shapes=[
            pltpu.VMEM((chips,) + block, jnp.float32),
            pltpu.VMEM((chips,) + block, jnp.bfloat16),
            pltpu.VMEM((chips,) + block, jnp.bfloat16),
            pltpu.VMEM(block, jnp.bfloat16),
            pltpu.VMEM(block, jnp.float32),
            dma((chips,)), dma((chips,)),
            dma((chips,)), dma((chips,)),
            dma((groups,)), dma((groups,)),
            dma((chips,)), dma((chips,)),
            dma((chips,)), dma((chips,)),
        ],
        compiler_params=pltpu.CompilerParams(
            collective_id=collective_id, has_side_effects=True, vmem_limit_bytes=32 * 2**20
        ),
        cost_estimate=pl.CostEstimate(
            flops=4 * rows * tokens, bytes_accessed=8 * rows * tokens, transcendentals=0
        ),
    )(x.reshape(shape))


def local(acts, target, proj_b, proj_a):
    toks, chans = lax.axis_size("tok"), lax.axis_size("chan")
    tok = lax.axis_index("tok")
    tokens, rank = acts.shape[0], proj_b.shape[0]
    factor_scale = -2.0 / (tokens * toks)
    acts_all = lax.all_gather(acts, "tok", axis=0, tiled=True)

    codes_part = lax.dot_general(
        proj_b, acts, (((1,), (1,)), ((), ())), preferred_element_type=jnp.float32
    )
    codes = reduce_gather(codes_part, chans, 1, 0).reshape(rank, tokens)
    predicted = lax.dot_general(
        codes, proj_a, (((0,), (1,)), ((), ())), preferred_element_type=jnp.float32
    )
    residual = (target.astype(jnp.float32) - predicted).astype(jnp.bfloat16)
    grad_part = lax.dot_general(
        proj_a, residual, (((0,), (1,)), ((), ())), preferred_element_type=jnp.float32
    )
    grad_codes = reduce_gather(grad_part, chans, toks, 1)

    share = rank // toks

    def term_a(step):
        rows = lax.dynamic_slice_in_dim(codes, (tok ^ step) * share, share, 0)
        return lax.dot_general(
            residual, rows, (((0,), (1,)), ((), ())), preferred_element_type=jnp.float32
        )

    grad_a = term_a(0)
    for step in range(1, toks):
        sent = lax.ppermute(
            term_a(step).astype(jnp.bfloat16), "tok", [(t, t ^ step) for t in range(toks)]
        )
        grad_a = grad_a + sent.astype(jnp.float32)

    grad_codes = grad_codes.reshape(toks, share, tokens).transpose(1, 0, 2)
    grad_b = jnp.dot(
        grad_codes.reshape(share, toks * tokens), acts_all, preferred_element_type=jnp.float32
    )
    return (grad_a * factor_scale, grad_b * factor_scale)


def solution(mesh):
    return jax.shard_map(
        local,
        mesh=mesh,
        in_specs=(P("tok", "chan"), P("tok", "chan"), P(None, "chan"), P("chan", None)),
        out_specs=(P("chan", "tok"), P("tok", "chan")),
        check_vma=False,
    )
```

```python
import functools

import jax
import jax.numpy as jnp
from jax import lax
from jax.experimental import pallas as pl
from jax.experimental.pallas import tpu as pltpu
from jax.sharding import PartitionSpec as P

MESH = pl.DeviceIdType.MESH


def reduce_gather_kernel(
    chips, groups, *refs
):
    if groups == 1:
        x_ref, out_ref = refs[:2]
        refs = refs[2:]
    else:
        codes_ref, a_ref, target_ref, out_ref, grad_ref = refs[:5]
        x_ref, res_ref, term_out, term_in, term_send, term_recv = refs[-6:]
        refs = refs[5:-6]
    (
        pair, mine, slots, reduced, total, pair_send, pair_recv, rs_send, rs_recv,
        tok_send, tok_recv, ag_send, ag_recv, fwd_send, fwd_recv,
    ) = refs
    me = lax.axis_index("chan")
    chip, core = me // 2, me % 2
    other = 1 - core
    partner = chip * 2 + other
    tok = lax.axis_index("tok")

    def peer(step):
        return lax.rem(chip + step, chips)

    def group(step):
        return tok ^ step

    barrier = pltpu.get_barrier_semaphore()
    pl.semaphore_signal(barrier, inc=1, device_id={"chan": partner}, device_id_type=MESH)
    for step in range(1, chips):
        pl.semaphore_signal(
            barrier, inc=1, device_id={"chan": peer(step) * 2 + core}, device_id_type=MESH
        )
    for step in range(1, groups):
        pl.semaphore_signal(barrier, inc=1, device_id={"tok": group(step)}, device_id_type=MESH)
    pl.semaphore_wait(barrier, chips + groups - 1)

    size = 256
    if groups > 1:
        @pl.loop(0, a_ref.shape[0] // size)
        def _(index):
            block = pl.ds(pl.multiple_of(index * size, size), size)
            predicted = jnp.dot(
                a_ref[block], codes_ref[...], preferred_element_type=jnp.float32
            )
            wanted = target_ref[:, block].astype(jnp.float32).T
            res_ref[block] = (wanted - predicted).astype(jnp.bfloat16)

    def make_x(side):
        rows = x_ref.shape[2] * x_ref.shape[3]

        @pl.loop(0, groups)
        def _(index):
            columns = pl.ds(pl.multiple_of((index * 2 + side) * rows, rows), rows)
            part = lax.dot_general(
                a_ref[:, columns], res_ref[...], (((0,), (0,)), ((), ())),
                preferred_element_type=jnp.float32,
            )
            x_ref[index, side] = part.reshape(x_ref.shape[2:])

    if groups > 1:
        make_x(other)

    order = [(chips // 2 + step) % chips for step in range(chips)]
    order = [step for step in order if step] + [0]

    def pair_copy(step):
        slot = peer(step)
        return pltpu.make_async_remote_copy(
            x_ref.at[:, other, slot], pair.at[slot], pair_send.at[slot], pair_recv.at[slot],
            device_id={"chan": partner}, device_id_type=MESH,
        )

    for step in order:
        pair_copy(step).start()

    if groups > 1:
        make_x(core)

    def rs_copy(step, landed):
        slot = peer(step)
        return pltpu.make_async_remote_copy(
            mine.at[slot], slots.at[landed], rs_send.at[slot], rs_recv.at[landed],
            device_id={"chan": slot * 2 + core}, device_id_type=MESH,
        )

    for step in order:
        slot = peer(step)
        pair_copy(step).wait_recv()
        value = x_ref[:, core, slot] + pair[slot]
        if step:
            mine[slot] = value.astype(jnp.bfloat16)
            rs_copy(step, chip).start()
        else:
            total[...] = value

    def term(step, block):
        share = grad_ref.shape[1]
        rows = codes_ref[pl.ds(pl.multiple_of(group(step) * share, share), share)]
        return lax.dot_general(
            res_ref[block], rows, (((1,), (1,)), ((), ())), preferred_element_type=jnp.float32
        )

    if groups > 1:

        @pl.loop(0, res_ref.shape[0] // size)
        def _(index):
            block = pl.ds(pl.multiple_of(index * size, size), size)
            for step in range(1, groups):
                term_out[step - 1, block] = term(step, block).astype(jnp.bfloat16)
            grad_ref[block] = term(0, block)

    for step in range(1, chips):
        slot = peer(step)
        rs_copy(step, slot).wait_recv()
        total[...] += slots[slot].astype(jnp.float32)

    if groups == 1:
        out_ref[:, core, chip] = total[...].astype(jnp.bfloat16)
    else:
        reduced[...] = total[...].astype(jnp.bfloat16)

        def tok_copy(step):
            target = group(step)
            return pltpu.make_async_remote_copy(
                reduced.at[target], out_ref.at[step, core, chip],
                tok_send.at[step], tok_recv.at[step],
                device_id={"tok": target}, device_id_type=MESH,
            )

        def term_copy(step):
            return pltpu.make_async_remote_copy(
                term_out.at[step - 1], term_in.at[step - 1],
                term_send.at[step - 1], term_recv.at[step - 1],
                device_id={"tok": group(step)}, device_id_type=MESH,
            )

        for step in range(1, groups):
            tok_copy(step).start()
        out_ref[0, core, chip] = reduced[tok]
        for step in range(1, groups):
            tok_copy(step).wait_recv()

    def ag_copy(step, landed):
        block = out_ref.at[:, core, landed]
        slot = peer(step)
        return pltpu.make_async_remote_copy(
            block, block, ag_send.at[slot], ag_recv.at[landed],
            device_id={"chan": slot * 2 + core}, device_id_type=MESH,
        )

    def fwd_copy(slot, side):
        block = out_ref.at[:, side, slot]
        return pltpu.make_async_remote_copy(
            block, block, fwd_send.at[slot], fwd_recv.at[slot],
            device_id={"chan": partner}, device_id_type=MESH,
        )

    for step in order[:-1]:
        ag_copy(step, chip).start()
    fwd_copy(chip, core).start()
    if groups > 1:
        for step in reversed(range(1, groups)):
            term_copy(step).start()
    for step in range(1, chips):
        slot = peer(step)
        ag_copy(step, slot).wait_recv()
        fwd_copy(slot, core).start()
    for step in range(chips):
        fwd_copy(peer(step), other).wait_recv()

    for step in range(chips):
        pair_copy(step).wait_send()
        fwd_copy(peer(step), core).wait_send()
        if step:
            rs_copy(step, chip).wait_send()
            ag_copy(step, chip).wait_send()
    if groups > 1:
        for step in range(1, groups):
            tok_copy(step).wait_send()
            term_copy(step).wait_send()
            term_copy(step).wait_recv()
            grad_ref[...] += term_in[step - 1].astype(jnp.float32)


def reduce_gather(operands, devices, groups, collective_id):
    rows, tokens = operands[0].shape
    chips = devices // 2
    part = rows // (devices * groups)
    shape = (groups, 2, chips, part, tokens)
    block = (groups, part, tokens)
    vmem = pl.BlockSpec(memory_space=pltpu.VMEM)
    dma = pltpu.SemaphoreType.DMA
    out_shape = [jax.ShapeDtypeStruct(shape, jnp.bfloat16)]
    extra, flops = [], 4 * rows * tokens
    if groups > 1:
        channels = operands[1].shape[0]
        term = (channels, rows // groups)
        out_shape.append(jax.ShapeDtypeStruct(term, jnp.float32))
        extra = [
            pltpu.VMEM(shape, jnp.float32),
            pltpu.VMEM((channels, tokens), jnp.bfloat16),
            pltpu.VMEM((groups - 1,) + term, jnp.bfloat16),
            pltpu.VMEM((groups - 1,) + term, jnp.bfloat16),
            dma((groups - 1,)), dma((groups - 1,)),
        ]
        flops = 6 * rows * tokens * channels
    else:
        operands = [operands[0].reshape(shape)]
    return pl.pallas_call(
        functools.partial(reduce_gather_kernel, chips, groups),
        out_shape=out_shape,
        in_specs=[vmem] * len(operands),
        out_specs=[vmem] * len(out_shape),
        scratch_shapes=[
            pltpu.VMEM((chips,) + block, jnp.float32),
            pltpu.VMEM((chips,) + block, jnp.bfloat16),
            pltpu.VMEM((chips,) + block, jnp.bfloat16),
            pltpu.VMEM(block, jnp.bfloat16),
            pltpu.VMEM(block, jnp.float32),
            dma((chips,)), dma((chips,)),
            dma((chips,)), dma((chips,)),
            dma((groups,)), dma((groups,)),
            dma((chips,)), dma((chips,)),
            dma((chips,)), dma((chips,)),
        ] + extra,
        compiler_params=pltpu.CompilerParams(
            collective_id=collective_id, has_side_effects=True, vmem_limit_bytes=48 * 2**20
        ),
        cost_estimate=pl.CostEstimate(
            flops=flops, bytes_accessed=8 * rows * tokens, transcendentals=0
        ),
    )(*operands)


def grad_b_kernel(places, scale, codes_ref, *refs):
    out_ref, total = refs[-1], None
    for (step, start), piece in zip(places, refs):
        term = jnp.dot(
            codes_ref[step, :, start : start + piece.shape[0]], piece[...],
            preferred_element_type=jnp.float32,
        )
        total = term if total is None else total + term
    out_ref[...] = total * scale


def grad_b_of(grad_codes, pieces, places, scale):
    share, columns = grad_codes.shape[1], pieces[0].shape[1]
    width = 512 if columns % 512 == 0 else 256
    tokens = sum(piece.shape[0] for piece in pieces)
    return pl.pallas_call(
        functools.partial(grad_b_kernel, places, scale),
        grid=(columns // width,),
        out_shape=jax.ShapeDtypeStruct((share, columns), jnp.float32),
        in_specs=[pl.BlockSpec(grad_codes.shape, lambda i: (0, 0, 0))]
        + [pl.BlockSpec((piece.shape[0], width), lambda i: (0, i)) for piece in pieces],
        out_specs=pl.BlockSpec((share, width), lambda i: (0, i)),
        compiler_params=pltpu.CompilerParams(vmem_limit_bytes=48 * 2**20),
        cost_estimate=pl.CostEstimate(
            flops=2 * share * columns * tokens,
            bytes_accessed=columns * (2 * tokens + 4 * share),
            transcendentals=0,
        ),
    )(grad_codes, *pieces)


def gather_start(acts, toks):
    if toks != 4:
        return [lax.all_gather(acts, "tok", axis=0, tiled=False)]
    return [
        lax.ppermute(acts, "tok", [(t, t ^ step) for t in range(toks)]) for step in (1, 2)
    ]


def gather_end(acts, begun, toks, tok):
    tokens = acts.shape[0]
    if toks != 4:
        (whole,) = begun
        pieces = [acts] + [
            lax.dynamic_index_in_dim(whole, tok ^ step, 0, keepdims=False)
            for step in range(1, toks)
        ]
        return [(step, 0) for step in range(toks)], pieces

    def move(x, step):
        return lax.ppermute(x, "tok", [(t, t ^ step) for t in range(toks)])

    half = tokens // 2
    along_x, along_y = begun
    low, high = move(along_x[:half], 2), move(along_y[half:], 1)
    return [(0, 0), (1, 0), (2, 0), (3, 0), (3, half)], [acts, along_x, along_y, low, high]


def local(acts, target, proj_b, proj_a):
    toks, chans = lax.axis_size("tok"), lax.axis_size("chan")
    tok = lax.axis_index("tok")
    tokens, rank = acts.shape[0], proj_b.shape[0]
    factor_scale = -2.0 / (tokens * toks)
    begun = gather_start(acts, toks)

    codes_part = lax.dot_general(
        proj_b, acts, (((1,), (1,)), ((), ())), preferred_element_type=jnp.float32
    )
    codes = reduce_gather([codes_part], chans, 1, 0)[0].reshape(rank, tokens)
    codes, begun = lax.optimization_barrier((codes, begun))
    places, pieces = gather_end(acts, begun, toks, tok)
    grad_codes, grad_a = reduce_gather([codes, proj_a, target], chans, toks, 1)
    grad_codes = grad_codes.reshape(toks, rank // toks, tokens)
    grad_b = grad_b_of(grad_codes, pieces, places, factor_scale)
    return (grad_a * factor_scale, grad_b)


def solution(mesh):
    return jax.shard_map(
        local,
        mesh=mesh,
        in_specs=(P("tok", "chan"), P("tok", "chan"), P(None, "chan"), P("chan", None)),
        out_specs=(P("chan", "tok"), P("tok", "chan")),
        check_vma=False,
    )
```

```python
import functools

import jax
import jax.numpy as jnp
from jax import lax
from jax.experimental import pallas as pl
from jax.experimental.pallas import tpu as pltpu
from jax.sharding import PartitionSpec as P

MESH = pl.DeviceIdType.MESH


def partners():
    me = lax.axis_index("chan")
    chip, core = me // 2, me % 2
    return chip, core, chip * 2 + 1 - core


def greet(chips, groups):
    chip, core, partner = partners()
    barrier = pltpu.get_barrier_semaphore()
    pl.semaphore_signal(barrier, inc=1, device_id={"chan": partner}, device_id_type=MESH)
    for step in range(1, chips):
        there = lax.rem(chip + step, chips) * 2 + core
        pl.semaphore_signal(barrier, inc=1, device_id={"chan": there}, device_id_type=MESH)
    for step in range(1, groups):
        there = lax.axis_index("tok") ^ step
        pl.semaphore_signal(barrier, inc=1, device_id={"tok": there}, device_id_type=MESH)
    pl.semaphore_wait(barrier, chips + groups - 1)


def reduce_phase(chips, x_ref, make_x, beside, refs):
    pair, mine, slots, total, pair_send, pair_recv, rs_send, rs_recv = refs
    chip, core, partner = partners()
    other = 1 - core

    def peer(step):
        return lax.rem(chip + step, chips)

    order = [(chips // 2 + step) % chips for step in range(chips)]
    order = [step for step in order if step] + [0]

    def pair_copy(step):
        slot = peer(step)
        return pltpu.make_async_remote_copy(
            x_ref.at[:, other, slot], pair.at[slot], pair_send.at[slot], pair_recv.at[slot],
            device_id={"chan": partner}, device_id_type=MESH,
        )

    def rs_copy(step, landed):
        slot = peer(step)
        return pltpu.make_async_remote_copy(
            mine.at[slot], slots.at[landed], rs_send.at[slot], rs_recv.at[landed],
            device_id={"chan": slot * 2 + core}, device_id_type=MESH,
        )

    make_x(other)
    for step in order:
        pair_copy(step).start()
    make_x(core)
    for step in order:
        slot = peer(step)
        pair_copy(step).wait_recv()
        value = x_ref[:, core, slot] + pair[slot]
        if step:
            mine[slot] = value.astype(jnp.bfloat16)
            rs_copy(step, chip).start()
        else:
            total[...] = value
    beside()
    for step in range(1, chips):
        slot = peer(step)
        rs_copy(step, slot).wait_recv()
        total[...] += slots[slot].astype(jnp.float32)
    for step in range(chips):
        pair_copy(step).wait_send()
        if step:
            rs_copy(step, chip).wait_send()


def gather_phase(chips, out_ref, refs):
    right_send, left_send, ag_recv, fwd_send, fwd_recv = refs
    chip, core, partner = partners()

    def hop(slot, right):
        block = out_ref.at[:, core, slot]
        there = lax.rem(chip + (1 if right else chips - 1), chips)
        return pltpu.make_async_remote_copy(
            block, block, (right_send if right else left_send).at[slot], ag_recv.at[slot],
            device_id={"chan": there * 2 + core}, device_id_type=MESH,
        )

    def fwd_copy(slot, side):
        block = out_ref.at[:, side, slot]
        return pltpu.make_async_remote_copy(
            block, block, fwd_send.at[slot], fwd_recv.at[slot],
            device_id={"chan": partner}, device_id_type=MESH,
        )

    has_right, has_left = chip + 1 < chips, chip > 0

    @pl.when(has_right)
    def _():
        hop(chip, True).start()

    @pl.when(has_left)
    def _():
        hop(chip, False).start()

    fwd_copy(chip, core).start()
    for step in range(1, chips):

        @pl.when(chip >= step)
        def _():
            hop(chip - step, True).wait_recv()

            @pl.when(has_right)
            def _():
                hop(chip - step, True).start()

            fwd_copy(chip - step, core).start()

        @pl.when(chip + step < chips)
        def _():
            hop(chip + step, False).wait_recv()

            @pl.when(has_left)
            def _():
                hop(chip + step, False).start()

            fwd_copy(chip + step, core).start()

    for slot in range(chips):
        fwd_copy(slot, 1 - core).wait_recv()
        fwd_copy(slot, core).wait_send()

        @pl.when(has_right & (slot <= chip))
        def _():
            hop(slot, True).wait_send()

        @pl.when(has_left & (slot >= chip))
        def _():
            hop(slot, False).wait_send()


def codes_kernel(chips, x_ref, out_ref, *refs):
    greet(chips, 1)
    reduce_phase(chips, x_ref, lambda side: None, lambda: None, refs[:8])
    chip, core, _ = partners()
    out_ref[:, core, chip] = refs[3][...].astype(jnp.bfloat16)
    gather_phase(chips, out_ref, refs[8:])


def gather_kernel(chips, piece_ref, out_ref, *refs):
    greet(chips, 1)
    chip, core, _ = partners()
    out_ref[:, core, chip] = piece_ref[...]
    gather_phase(chips, out_ref, refs)


def term_place(groups, step, half):
    if groups != 4:
        return step - 1, half
    return {(1, 0): (0, 0), (3, 0): (0, 1), (2, 1): (1, 0), (3, 1): (1, 1),
            (2, 0): (2, 0), (1, 1): (2, 1)}[step, half]


def grads_kernel(chips, groups, codes_ref, a_ref, target_ref, piece_ref, own_ref, *refs):
    terms, refs = refs[: groups - 1], refs[groups - 1 :]
    x_ref, res_ref, reduced, tok_send, tok_recv = refs[8:]
    total = refs[3]
    tok = lax.axis_index("tok")
    greet(chips, groups)
    size = 256

    @pl.loop(0, a_ref.shape[0] // size)
    def _(index):
        block = pl.ds(pl.multiple_of(index * size, size), size)
        predicted = jnp.dot(a_ref[block], codes_ref[...], preferred_element_type=jnp.float32)
        wanted = target_ref[:, block].astype(jnp.float32).T
        res_ref[block] = (wanted - predicted).astype(jnp.bfloat16)

    def make_x(side):
        rows = x_ref.shape[2] * x_ref.shape[3]

        @pl.loop(0, groups)
        def _(index):
            columns = pl.ds(pl.multiple_of((index * 2 + side) * rows, rows), rows)
            part = lax.dot_general(
                a_ref[:, columns], res_ref[...], (((0,), (0,)), ((), ())),
                preferred_element_type=jnp.float32,
            )
            x_ref[index, side] = part.reshape(x_ref.shape[2:])

    def term(step, block):
        share = own_ref.shape[1]
        rows = codes_ref[pl.ds(pl.multiple_of((tok ^ step) * share, share), share)]
        return lax.dot_general(
            res_ref[block], rows, (((1,), (1,)), ((), ())), preferred_element_type=jnp.float32
        )

    def make_terms():
        length = terms[0].shape[1]
        chunk = min(size, length)
        for half in range(2):

            @pl.loop(0, length // chunk)
            def _(index):
                start = pl.multiple_of(index * chunk, chunk)
                block = pl.ds(pl.multiple_of(half * length + start, chunk), chunk)
                for step in range(1, groups):
                    array, place = term_place(groups, step, half)
                    value = term(step, block).astype(jnp.bfloat16)
                    terms[array][place, pl.ds(start, chunk)] = value
                own_ref[block] = term(0, block)

    reduce_phase(chips, x_ref, make_x, make_terms, refs[:8])
    reduced[...] = total[...].astype(jnp.bfloat16)

    def tok_copy(step):
        return pltpu.make_async_remote_copy(
            reduced.at[tok ^ step], piece_ref.at[step], tok_send.at[step], tok_recv.at[step],
            device_id={"tok": tok ^ step}, device_id_type=MESH,
        )

    for step in range(1, groups):
        tok_copy(step).start()
    piece_ref[0] = reduced[tok]
    for step in range(1, groups):
        tok_copy(step).wait_recv()
        tok_copy(step).wait_send()


def call(kernel, collective_id, operands, out_shape, scratch):
    vmem = pl.BlockSpec(memory_space=pltpu.VMEM)
    return pl.pallas_call(
        kernel,
        out_shape=out_shape,
        in_specs=[vmem] * len(operands),
        out_specs=[vmem] * len(out_shape),
        scratch_shapes=scratch,
        compiler_params=pltpu.CompilerParams(
            collective_id=collective_id, has_side_effects=True, vmem_limit_bytes=48 * 2**20
        ),
        cost_estimate=pl.CostEstimate(flops=0, bytes_accessed=1024, transcendentals=0),
    )(*operands)


def reduce_scratch(chips, block):
    dma = pltpu.SemaphoreType.DMA((chips,))
    return [
        pltpu.VMEM((chips,) + block, jnp.float32),
        pltpu.VMEM((chips,) + block, jnp.bfloat16),
        pltpu.VMEM((chips,) + block, jnp.bfloat16),
        pltpu.VMEM(block, jnp.float32),
    ] + [dma] * 4


def sum_codes(x, devices):
    rows, tokens = x.shape
    chips = devices // 2
    shape = (1, 2, chips, rows // devices, tokens)
    out = call(
        functools.partial(codes_kernel, chips), 0, [x.reshape(shape)],
        [jax.ShapeDtypeStruct(shape, jnp.bfloat16)],
        reduce_scratch(chips, (1,) + shape[3:]) + [pltpu.SemaphoreType.DMA((chips,))] * 5,
    )
    return out[0].reshape(rows, tokens)


def gather_codes(piece, devices):
    groups, part, tokens = piece.shape
    chips = devices // 2
    shape = (groups, 2, chips, part, tokens)
    out = call(
        functools.partial(gather_kernel, chips), 2, [piece],
        [jax.ShapeDtypeStruct(shape, jnp.bfloat16)],
        [pltpu.SemaphoreType.DMA((chips,))] * 5,
    )
    return out[0].reshape(groups, devices * part, tokens)


def grads(codes, proj_a, target, devices, groups):
    rows, tokens = codes.shape
    channels, chips = proj_a.shape[0], devices // 2
    block = (groups, rows // (devices * groups), tokens)
    share = rows // groups
    dma = pltpu.SemaphoreType.DMA((groups,))
    out = call(
        functools.partial(grads_kernel, chips, groups), 1, [codes, proj_a, target],
        [
            jax.ShapeDtypeStruct(block, jnp.bfloat16),
            jax.ShapeDtypeStruct((channels, share), jnp.float32),
        ]
        + [jax.ShapeDtypeStruct((2, channels // 2, share), jnp.bfloat16)] * (groups - 1),
        reduce_scratch(chips, block)
        + [
            pltpu.VMEM((groups, 2, chips) + block[1:], jnp.float32),
            pltpu.VMEM((channels, tokens), jnp.bfloat16),
            pltpu.VMEM(block, jnp.bfloat16),
            dma, dma,
        ],
    )
    return out[0], out[1], out[2:]


def grad_b_kernel(places, scale, codes_ref, *refs):
    out_ref, total = refs[-1], None
    for (step, start), piece in zip(places, refs):
        term = jnp.dot(
            codes_ref[step, :, start : start + piece.shape[0]], piece[...],
            preferred_element_type=jnp.float32,
        )
        total = term if total is None else total + term
    out_ref[...] = total * scale


def grad_b_of(grad_codes, pieces, places, scale):
    share, columns = grad_codes.shape[1], pieces[0].shape[1]
    width = 512 if columns % 512 == 0 else 256
    tokens = sum(piece.shape[0] for piece in pieces)
    return pl.pallas_call(
        functools.partial(grad_b_kernel, places, scale),
        grid=(columns // width,),
        out_shape=jax.ShapeDtypeStruct((share, columns), jnp.float32),
        in_specs=[pl.BlockSpec(grad_codes.shape, lambda i: (0, 0, 0))]
        + [pl.BlockSpec((piece.shape[0], width), lambda i: (0, i)) for piece in pieces],
        out_specs=pl.BlockSpec((share, width), lambda i: (0, i)),
        compiler_params=pltpu.CompilerParams(vmem_limit_bytes=48 * 2**20),
        cost_estimate=pl.CostEstimate(
            flops=2 * share * columns * tokens,
            bytes_accessed=columns * (2 * tokens + 4 * share),
            transcendentals=0,
        ),
    )(grad_codes, *pieces)


def gather_start(acts, toks):
    if toks != 4:
        return [lax.all_gather(acts, "tok", axis=0, tiled=False)]
    return [
        lax.ppermute(acts, "tok", [(t, t ^ step) for t in range(toks)]) for step in (1, 2)
    ]


def gather_end(acts, begun, toks, tok):
    tokens = acts.shape[0]
    if toks != 4:
        (whole,) = begun
        pieces = [acts] + [
            lax.dynamic_index_in_dim(whole, tok ^ step, 0, keepdims=False)
            for step in range(1, toks)
        ]
        return [(step, 0) for step in range(toks)], pieces

    def move(x, step):
        return lax.ppermute(x, "tok", [(t, t ^ step) for t in range(toks)])

    half = tokens // 2
    along_x, along_y = begun
    low, high = move(along_x[:half], 2), move(along_y[half:], 1)
    return [(0, 0), (1, 0), (2, 0), (3, 0), (3, half)], [acts, along_x, along_y, low, high]


def local(acts, target, proj_b, proj_a):
    toks, chans = lax.axis_size("tok"), lax.axis_size("chan")
    tok = lax.axis_index("tok")
    tokens, rank = acts.shape[0], proj_b.shape[0]
    factor_scale = -2.0 / (tokens * toks)
    begun = gather_start(acts, toks)

    codes_part = lax.dot_general(
        proj_b, acts, (((1,), (1,)), ((), ())), preferred_element_type=jnp.float32
    )
    codes = sum_codes(codes_part, chans)
    codes, begun = lax.optimization_barrier((codes, begun))
    places, pieces = gather_end(acts, begun, toks, tok)
    piece, own, terms = grads(codes, proj_a, target, chans, toks)

    def move(x, step):
        return lax.ppermute(x, "tok", [(t, t ^ step) for t in range(toks)])

    if toks == 4:
        from_x, from_y = move(terms[0], 1), move(terms[1], 2)
    else:
        first = [move(value, step + 1) for step, value in enumerate(terms)]
    grad_codes = gather_codes(piece, chans)
    if toks == 4:
        grad_codes, from_x, from_y = lax.optimization_barrier((grad_codes, from_x, from_y))
        to_y = terms[2][0].astype(jnp.float32) + from_x[1].astype(jnp.float32)
        to_x = terms[2][1].astype(jnp.float32) + from_y[1].astype(jnp.float32)
        low, high = move(to_y.astype(jnp.bfloat16), 2), move(to_x.astype(jnp.bfloat16), 1)
        grad_b = grad_b_of(grad_codes, pieces, places, factor_scale)
        grad_b, low, high = lax.optimization_barrier((grad_b, low, high))
        low, high = low.astype(jnp.float32), high.astype(jnp.float32)
        grad_a = own + jnp.concatenate(
            [from_x[0].astype(jnp.float32) + low, from_y[0].astype(jnp.float32) + high]
        )
    else:
        grad_a = own + sum(value.reshape(own.shape).astype(jnp.float32) for value in first)
        grad_b = grad_b_of(grad_codes, pieces, places, factor_scale)
    return (grad_a * factor_scale, grad_b)


def solution(mesh):
    return jax.shard_map(
        local,
        mesh=mesh,
        in_specs=(P("tok", "chan"), P("tok", "chan"), P(None, "chan"), P("chan", None)),
        out_specs=(P("chan", "tok"), P("tok", "chan")),
        check_vma=False,
    )
```

```python
import functools

import jax
import jax.numpy as jnp
from jax import lax
from jax.experimental import pallas as pl
from jax.experimental.pallas import tpu as pltpu
from jax.sharding import PartitionSpec as P

MESH = pl.DeviceIdType.MESH


def partners():
    me = lax.axis_index("chan")
    chip, core = me // 2, me % 2
    return chip, core, chip * 2 + 1 - core


def greet(chips, groups):
    chip, core, partner = partners()
    barrier = pltpu.get_barrier_semaphore()
    pl.semaphore_signal(barrier, inc=1, device_id={"chan": partner}, device_id_type=MESH)
    for step in range(1, chips):
        there = lax.rem(chip + step, chips) * 2 + core
        pl.semaphore_signal(barrier, inc=1, device_id={"chan": there}, device_id_type=MESH)
    for step in range(1, groups):
        there = lax.axis_index("tok") ^ step
        pl.semaphore_signal(barrier, inc=1, device_id={"tok": there}, device_id_type=MESH)
    pl.semaphore_wait(barrier, chips + groups - 1)


def reduce_phase(chips, x_ref, make_x, beside, refs):
    pair, mine, slots, total, pair_send, pair_recv, rs_send, rs_recv = refs
    chip, core, partner = partners()
    other = 1 - core

    def peer(step):
        return lax.rem(chip + step, chips)

    order = [(chips // 2 + step) % chips for step in range(chips)]
    order = [step for step in order if step] + [0]

    def pair_copy(step):
        slot = peer(step)
        return pltpu.make_async_remote_copy(
            x_ref.at[:, other, slot], pair.at[slot], pair_send.at[slot], pair_recv.at[slot],
            device_id={"chan": partner}, device_id_type=MESH,
        )

    def rs_copy(step, landed):
        slot = peer(step)
        return pltpu.make_async_remote_copy(
            mine.at[slot], slots.at[landed], rs_send.at[slot], rs_recv.at[landed],
            device_id={"chan": slot * 2 + core}, device_id_type=MESH,
        )

    make_x(other)
    for step in order:
        pair_copy(step).start()
    make_x(core)
    for step in order:
        slot = peer(step)
        pair_copy(step).wait_recv()
        value = x_ref[:, core, slot] + pair[slot]
        if step:
            mine[slot] = value.astype(jnp.bfloat16)
            rs_copy(step, chip).start()
        else:
            total[...] = value
    beside()
    for step in range(1, chips):
        slot = peer(step)
        rs_copy(step, slot).wait_recv()
        total[...] += slots[slot].astype(jnp.float32)
    for step in range(chips):
        pair_copy(step).wait_send()
        if step:
            rs_copy(step, chip).wait_send()


def gather_phase(chips, out_ref, refs):
    right_send, left_send, ag_recv, fwd_send, fwd_recv = refs
    chip, core, partner = partners()

    def hop(slot, right):
        block = out_ref.at[:, core, slot]
        there = lax.rem(chip + (1 if right else chips - 1), chips)
        return pltpu.make_async_remote_copy(
            block, block, (right_send if right else left_send).at[slot], ag_recv.at[slot],
            device_id={"chan": there * 2 + core}, device_id_type=MESH,
        )

    def fwd_copy(slot, side):
        block = out_ref.at[:, side, slot]
        return pltpu.make_async_remote_copy(
            block, block, fwd_send.at[slot], fwd_recv.at[slot],
            device_id={"chan": partner}, device_id_type=MESH,
        )

    has_right, has_left = chip + 1 < chips, chip > 0

    @pl.when(has_right)
    def _():
        hop(chip, True).start()

    @pl.when(has_left)
    def _():
        hop(chip, False).start()

    fwd_copy(chip, core).start()
    for step in range(1, chips):

        @pl.when(chip >= step)
        def _():
            hop(chip - step, True).wait_recv()

            @pl.when(has_right)
            def _():
                hop(chip - step, True).start()

            fwd_copy(chip - step, core).start()

        @pl.when(chip + step < chips)
        def _():
            hop(chip + step, False).wait_recv()

            @pl.when(has_left)
            def _():
                hop(chip + step, False).start()

            fwd_copy(chip + step, core).start()

    for slot in range(chips):
        fwd_copy(slot, 1 - core).wait_recv()
        fwd_copy(slot, core).wait_send()

        @pl.when(has_right & (slot <= chip))
        def _():
            hop(slot, True).wait_send()

        @pl.when(has_left & (slot >= chip))
        def _():
            hop(slot, False).wait_send()


def codes_kernel(chips, x_ref, out_ref, *refs):
    greet(chips, 1)
    reduce_phase(chips, x_ref, lambda side: None, lambda: None, refs[:8])
    chip, core, _ = partners()
    out_ref[:, core, chip] = refs[3][...].astype(jnp.bfloat16)
    gather_phase(chips, out_ref, refs[8:])


def gather_kernel(chips, piece_ref, out_ref, *refs):
    greet(chips, 1)
    chip, core, _ = partners()
    out_ref[:, core, chip] = piece_ref[...]
    gather_phase(chips, out_ref, refs)


def term_place(groups, step, half):
    if groups != 4:
        return step - 1, half
    return {(1, 0): (0, 0), (3, 0): (0, 1), (2, 1): (1, 0), (3, 1): (1, 1),
            (2, 0): (2, 0), (1, 1): (2, 1)}[step, half]


def grads_kernel(chips, groups, codes_ref, a_ref, target_ref, piece_ref, own_ref, *refs):
    terms, refs = refs[: groups - 1], refs[groups - 1 :]
    x_ref, res_ref, reduced, tok_send, tok_recv = refs[8:]
    total = refs[3]
    tok = lax.axis_index("tok")
    greet(chips, groups)
    size = 256

    @pl.loop(0, a_ref.shape[0] // size)
    def _(index):
        block = pl.ds(pl.multiple_of(index * size, size), size)
        predicted = jnp.dot(a_ref[block], codes_ref[...], preferred_element_type=jnp.float32)
        wanted = target_ref[:, block].astype(jnp.float32).T
        res_ref[block] = (wanted - predicted).astype(jnp.bfloat16)

    def make_x(side):
        rows = x_ref.shape[2] * x_ref.shape[3]

        @pl.loop(0, groups)
        def _(index):
            columns = pl.ds(pl.multiple_of((index * 2 + side) * rows, rows), rows)
            part = lax.dot_general(
                a_ref[:, columns], res_ref[...], (((0,), (0,)), ((), ())),
                preferred_element_type=jnp.float32,
            )
            x_ref[index, side] = part.reshape(x_ref.shape[2:])

    def term(step, block):
        share = own_ref.shape[1]
        rows = codes_ref[pl.ds(pl.multiple_of((tok ^ step) * share, share), share)]
        return lax.dot_general(
            res_ref[block], rows, (((1,), (1,)), ((), ())), preferred_element_type=jnp.float32
        )

    def make_terms():
        length = terms[0].shape[1]
        chunk = min(size, length)
        for half in range(2):

            @pl.loop(0, length // chunk)
            def _(index):
                start = pl.multiple_of(index * chunk, chunk)
                block = pl.ds(pl.multiple_of(half * length + start, chunk), chunk)
                for step in range(1, groups):
                    array, place = term_place(groups, step, half)
                    value = term(step, block).astype(jnp.bfloat16)
                    terms[array][place, pl.ds(start, chunk)] = value
                own_ref[block] = term(0, block)

    reduce_phase(chips, x_ref, make_x, make_terms, refs[:8])
    reduced[...] = total[...].astype(jnp.bfloat16)

    def tok_copy(step):
        return pltpu.make_async_remote_copy(
            reduced.at[tok ^ step], piece_ref.at[step], tok_send.at[step], tok_recv.at[step],
            device_id={"tok": tok ^ step}, device_id_type=MESH,
        )

    for step in range(1, groups):
        tok_copy(step).start()
    piece_ref[0] = reduced[tok]
    for step in range(1, groups):
        tok_copy(step).wait_recv()
        tok_copy(step).wait_send()


def call(kernel, collective_id, operands, out_shape, scratch):
    vmem = pl.BlockSpec(memory_space=pltpu.VMEM)
    return pl.pallas_call(
        kernel,
        out_shape=out_shape,
        in_specs=[vmem] * len(operands),
        out_specs=[vmem] * len(out_shape),
        scratch_shapes=scratch,
        compiler_params=pltpu.CompilerParams(
            collective_id=collective_id, has_side_effects=True, vmem_limit_bytes=48 * 2**20
        ),
        cost_estimate=pl.CostEstimate(flops=0, bytes_accessed=1024, transcendentals=0),
    )(*operands)


def reduce_scratch(chips, block):
    dma = pltpu.SemaphoreType.DMA((chips,))
    return [
        pltpu.VMEM((chips,) + block, jnp.float32),
        pltpu.VMEM((chips,) + block, jnp.bfloat16),
        pltpu.VMEM((chips,) + block, jnp.bfloat16),
        pltpu.VMEM(block, jnp.float32),
    ] + [dma] * 4


def sum_codes(x, devices):
    rows, tokens = x.shape
    chips = devices // 2
    shape = (1, 2, chips, rows // devices, tokens)
    out = call(
        functools.partial(codes_kernel, chips), 0, [x.reshape(shape)],
        [jax.ShapeDtypeStruct(shape, jnp.bfloat16)],
        reduce_scratch(chips, (1,) + shape[3:]) + [pltpu.SemaphoreType.DMA((chips,))] * 5,
    )
    return out[0].reshape(rows, tokens)


def gather_codes(piece, devices):
    groups, part, tokens = piece.shape
    chips = devices // 2
    shape = (groups, 2, chips, part, tokens)
    out = call(
        functools.partial(gather_kernel, chips), 2, [piece],
        [jax.ShapeDtypeStruct(shape, jnp.bfloat16)],
        [pltpu.SemaphoreType.DMA((chips,))] * 5,
    )
    return out[0].reshape(groups, devices * part, tokens)


def grads(codes, proj_a, target, devices, groups):
    rows, tokens = codes.shape
    channels, chips = proj_a.shape[0], devices // 2
    block = (groups, rows // (devices * groups), tokens)
    share = rows // groups
    dma = pltpu.SemaphoreType.DMA((groups,))
    out = call(
        functools.partial(grads_kernel, chips, groups), 1, [codes, proj_a, target],
        [
            jax.ShapeDtypeStruct(block, jnp.bfloat16),
            jax.ShapeDtypeStruct((channels, share), jnp.float32),
        ]
        + [jax.ShapeDtypeStruct((2, channels // 2, share), jnp.bfloat16)] * (groups - 1),
        reduce_scratch(chips, block)
        + [
            pltpu.VMEM((groups, 2, chips) + block[1:], jnp.float32),
            pltpu.VMEM((channels, tokens), jnp.bfloat16),
            pltpu.VMEM(block, jnp.bfloat16),
            dma, dma,
        ],
    )
    return out[0], out[1], out[2:]


def grad_b_kernel(places, scale, codes_ref, *refs):
    out_ref, total = refs[-1], None
    for (step, start), piece in zip(places, refs):
        term = jnp.dot(
            codes_ref[step, :, start : start + piece.shape[0]], piece[...],
            preferred_element_type=jnp.float32,
        )
        total = term if total is None else total + term
    out_ref[...] = total * scale


def grad_b_of(grad_codes, pieces, places, scale):
    share, columns = grad_codes.shape[1], pieces[0].shape[1]
    width = 512 if columns % 512 == 0 else 256
    tokens = sum(piece.shape[0] for piece in pieces)
    return pl.pallas_call(
        functools.partial(grad_b_kernel, places, scale),
        grid=(columns // width,),
        out_shape=jax.ShapeDtypeStruct((share, columns), jnp.float32),
        in_specs=[pl.BlockSpec(grad_codes.shape, lambda i: (0, 0, 0))]
        + [pl.BlockSpec((piece.shape[0], width), lambda i: (0, i)) for piece in pieces],
        out_specs=pl.BlockSpec((share, width), lambda i: (0, i)),
        compiler_params=pltpu.CompilerParams(vmem_limit_bytes=48 * 2**20),
        cost_estimate=pl.CostEstimate(
            flops=2 * share * columns * tokens,
            bytes_accessed=columns * (2 * tokens + 4 * share),
            transcendentals=0,
        ),
    )(grad_codes, *pieces)


def move(x, step):
    toks = lax.axis_size("tok")
    return lax.ppermute(x, "tok", [(t, t ^ step) for t in range(toks)])


def gather_start(acts, toks):
    if toks != 4:
        return [lax.all_gather(acts, "tok", axis=0, tiled=False)]
    half = acts.shape[0] // 2
    return [move(acts[:half], 1), move(acts[half:], 2)]


def gather_next(acts, toks):
    if toks != 4:
        return []
    half = acts.shape[0] // 2
    return [move(acts[half:], 1), move(acts[:half], 2)]


def gather_end(acts, begun, rest, toks, tok):
    half = acts.shape[0] // 2
    if toks != 4:
        (whole,) = begun
        pieces = [acts] + [
            lax.dynamic_index_in_dim(whole, tok ^ step, 0, keepdims=False)
            for step in range(1, toks)
        ]
        return [(step, 0) for step in range(toks)], pieces
    x_low, y_high = begun
    x_high, y_low = rest
    places = [(0, 0), (1, 0), (1, half), (2, 0), (2, half), (3, 0), (3, half)]
    return places, [acts, x_low, x_high, y_low, y_high, move(x_low, 2), move(y_high, 1)]


def local(acts, target, proj_b, proj_a):
    toks, chans = lax.axis_size("tok"), lax.axis_size("chan")
    tok = lax.axis_index("tok")
    tokens, rank = acts.shape[0], proj_b.shape[0]
    factor_scale = -2.0 / (tokens * toks)
    begun = gather_start(acts, toks)

    codes_part = lax.dot_general(
        proj_b, acts, (((1,), (1,)), ((), ())), preferred_element_type=jnp.float32
    )
    late, codes_part = lax.optimization_barrier((acts, codes_part))
    rest = gather_next(late, toks)
    codes = sum_codes(codes_part, chans)
    codes, begun = lax.optimization_barrier((codes, begun))
    places, pieces = gather_end(acts, begun, rest, toks, tok)
    piece, own, terms = grads(codes, proj_a, target, chans, toks)

    if toks == 4:
        from_x, from_y = move(terms[0], 1), move(terms[1], 2)
    else:
        first = [move(value, step + 1) for step, value in enumerate(terms)]
    if toks == 4:
        piece, pieces[2], pieces[3] = lax.optimization_barrier((piece, pieces[2], pieces[3]))
    grad_codes = gather_codes(piece, chans)
    if toks == 4:
        grad_codes, from_x, from_y = lax.optimization_barrier((grad_codes, from_x, from_y))
        to_y = terms[2][0].astype(jnp.float32) + from_x[1].astype(jnp.float32)
        to_x = terms[2][1].astype(jnp.float32) + from_y[1].astype(jnp.float32)
        low, high = move(to_y.astype(jnp.bfloat16), 2), move(to_x.astype(jnp.bfloat16), 1)
        grad_b = grad_b_of(grad_codes, pieces, places, factor_scale)
        grad_b, low, high = lax.optimization_barrier((grad_b, low, high))
        low, high = low.astype(jnp.float32), high.astype(jnp.float32)
        grad_a = own + jnp.concatenate(
            [from_x[0].astype(jnp.float32) + low, from_y[0].astype(jnp.float32) + high]
        )
    else:
        grad_a = own + sum(value.reshape(own.shape).astype(jnp.float32) for value in first)
        grad_b = grad_b_of(grad_codes, pieces, places, factor_scale)
    return (grad_a * factor_scale, grad_b)


def solution(mesh):
    return jax.shard_map(
        local,
        mesh=mesh,
        in_specs=(P("tok", "chan"), P("tok", "chan"), P(None, "chan"), P("chan", None)),
        out_specs=(P("chan", "tok"), P("tok", "chan")),
        check_vma=False,
    )
```
